32 devices in a mesh: section: 4 (over x, core), expert: 4 (over z), dp: 2 (over y).
Axes of the slice: x: 2, y: 2, z: 4, core: 2. Of those that a mesh axis runs over, the one named last changes fastest.
Arguments:
- tokens: bfloat16 [2, 512, 3072], P(None, ('expert', 'dp')), may hold values from -6 to 6
- routes: int32 [2, 512, 2], P(None, ('expert', 'dp')), may hold values from 0 to 3, all different within a row; in each aligned block of 64 rows (0 to 63, 64 to 127, ..., all dimensions but the last counted through in order) at most 36 rows name the same one
- router: bfloat16 [3072, 4], replicated, may hold values from -0.109375 to 0.109375
- gate_weight: bfloat16 [4, 8192, 3072], P('expert', ('section', 'dp')), may hold values from -0.109375 to 0.109375
- up_weight: bfloat16 [4, 8192, 3072], P('expert', ('section', 'dp')), may hold values from -0.109375 to 0.109375
- down_weight: bfloat16 [4, 8192, 3072], P('expert', ('section', 'dp')), may hold values from -0.0625 to 0.0625
Outputs:
- activations: bfloat16 [2, 512, 3072], P(None, ('expert', 'dp'), 'section')
- gram: bfloat16 [4, 3072, 3072], P('expert', ('section', 'dp'))
The draws below stay inside these ranges and needn't reach their ends.
Inputs may be any that keep to these rules, and one draw needn't show every extreme that they name: `routes`: in every micro-batch, each aligned block of 64 tokens (the tokens of one device) names no expert more than 36 times, a bound that some block reaches; the two experts of a token differ; every expert is named somewhere.
All inputs are finite; a program needn't handle non-finite values.
Results may differ from the reference program's by a relative error of at most 0.02.
Values may be sent and summed in bfloat16 or wider, within the bound.
A program may use at most 128 MiB of HBM per device.

```python
import math
import jax
import jax.numpy as jnp
import numpy as np
from jax import lax

D = 3072
FW = 8192
MB = 2
TOK_DEV = 64
EXPERTS = 4
CAP = 36
TOKENS = 512
N_EXPERT = 4
N_DP = 2


def levels(key, extent, split, least, high):
    loudness, own = 1.0, jax.random.fold_in(key, 6)
    for position, blocks in split:
        draws = jnp.exp(jax.random.uniform(jax.random.fold_in(own, position), (blocks,), jnp.float32, least / len(split), high / len(split)))
        loudness = loudness * jnp.repeat(draws, extent[position] // blocks).reshape([-1 if axis == position else 1 for axis in range(len(extent))])
    return loudness


def shared_out(stream_key, own, number, rows, count, top, reach, lean):
    order = jax.random.permutation(stream_key, count)
    crowded, ordinary = shares(count, rows * top, reach, lean, True), shares(count, rows * top, reach, lean, False)
    places = jnp.arange(count)

    def named(sizes, rotation):
        used = int((sizes > 0).sum())
        fixed = max(1, used // 4)
        passed = fixed + (places - fixed + rotation * (used - fixed)) % max(1, count - fixed)
        return jnp.zeros((count,), jnp.int32).at[order[jnp.where(places < fixed, places, passed)]].set(jnp.asarray(sizes, jnp.int32))

    sizes = jnp.where(number % 4 == 0, named(crowded, number // 4), named(ordinary, number - number // 4 - 1))
    mixed = jax.random.permutation(jax.random.fold_in(own, 3), count)
    source_of, receiver = mixed[0:count // 2 * 2:2], mixed[1:count // 2 * 2:2]
    room = jnp.minimum(sizes[source_of] - 1, reach - sizes[receiver]) // 2
    room = jnp.where((source_of == order[0]) | (receiver == order[0]) | (sizes[receiver] == 0), 0, jnp.maximum(room, 0))
    passed = jax.random.randint(jax.random.fold_in(own, 4), (count // 2,), 0, 1 << 20) % (room + 1)
    sizes = sizes.at[source_of].add(-passed).at[receiver].add(passed)
    members = jnp.searchsorted(jnp.cumsum(sizes), jnp.arange(rows * top), side="right").astype(jnp.int32)
    table = members.reshape(top, rows).T
    table = table[jax.random.permutation(jax.random.fold_in(own, 1), rows)]
    rotation = jax.random.randint(jax.random.fold_in(own, 2), (rows, 1), 0, top)
    return jnp.take_along_axis(table, (jnp.arange(top)[None, :] + rotation) % top, axis=1)


def shares(number_of, total, bound, skew, full):
    weights = [(1 << 20) // math.isqrt(grade ** skew) + 1 for grade in range(1, number_of + 1)]
    largest = bound if full else min(bound, max(-(-total // number_of), total * weights[0] // sum(weights)))
    least = 1 if total - largest >= number_of - 1 else 0
    holding, surplus = [largest] + [least] * (number_of - 1), total - largest - least * (number_of - 1)
    while surplus > 0:
        candidates = [i for i in range(1, number_of) if holding[i] < largest] or [i for i in range(1, number_of) if holding[i] < bound]
        pool, left = sum([weights[i] for i in candidates]), surplus
        for i in candidates:
            more = min(bound - holding[i], max(1, left * weights[i] // pool), surplus)
            holding[i] = holding[i] + more
            surplus = surplus - more
    return np.array(holding)


def scatter_about(rng, shape, spread, limit, shards=(), kind=jnp.bfloat16):
    entries = jax.random.normal(rng, shape, jnp.float32) * spread
    if len(shards) > 0:
        entries = levels(rng, shape, shards, -0.22, 0.18) * entries
    return jnp.clip(entries, min=-limit, max=limit).astype(kind)


def setup_inputs(seed: int = 0) -> dict:
    key_of = jax.random.split(jax.random.key(seed), 7)
    tokens = scatter_about(key_of[0], (MB, TOKENS, D), 1.0, 6.0, ((1, 8),))
    routes_keys = jax.random.split(jax.random.fold_in(key_of[1], 1), MB * TOKENS // TOK_DEV)
    routes_turns = jax.random.permutation(jax.random.fold_in(key_of[1], 3), MB * TOKENS // TOK_DEV)
    routes = jax.vmap(lambda own, number: shared_out(jax.random.fold_in(key_of[1], 2), own, number, TOK_DEV, EXPERTS, 2, CAP, 2))(routes_keys, routes_turns).reshape((MB, TOKENS, 2))
    router = scatter_about(key_of[2], (D, EXPERTS), D ** -0.5, 0.109375)
    gate_weight = scatter_about(key_of[3], (EXPERTS, FW, D), D ** -0.5, 0.109375, ((0, 4), (1, 8)))
    up_weight = scatter_about(key_of[4], (EXPERTS, FW, D), D ** -0.5, 0.109375, ((0, 4), (1, 8)))
    down_weight = scatter_about(key_of[5], (EXPERTS, FW, D), FW ** -0.5, 0.0625, ((0, 4), (1, 8)))
    return {"tokens": tokens, "routes": routes, "router": router, "gate_weight": gate_weight, "up_weight": up_weight, "down_weight": down_weight}


def route_targets(route_ids, experts, capacity):
    onehot = (route_ids[:, :, None] == jnp.arange(experts, dtype=jnp.int32)[None, None, :]).astype(jnp.int32)
    flattened = onehot.reshape(-1, experts)
    before = jnp.cumsum(flattened, axis=0) - flattened
    slot_rank = jnp.sum(before * flattened, axis=1).reshape(route_ids.shape)
    return (route_ids * capacity + slot_rank).astype(jnp.int32)


def expert_pass(operands):
    inputs, gate_w, up_w, down_w = operands
    as_float = inputs.astype(jnp.float32)
    gate_part = lax.dot_general(as_float, gate_w.astype(jnp.float32), (((1,), (1,)), ((), ())))
    up_part = lax.dot_general(as_float, up_w.astype(jnp.float32), (((1,), (1,)), ((), ())))
    hidden_units = (jax.nn.silu(gate_part) * up_part).astype(jnp.bfloat16)
    return jnp.dot(hidden_units.astype(jnp.float32), down_w.astype(jnp.float32)).astype(jnp.bfloat16)


def reference(tokens, routes, router, gate_weight, up_weight, down_weight):
    experts = EXPERTS
    capacity = CAP
    groups = N_EXPERT * N_DP
    blocks = MB * groups
    logits = jnp.einsum("mtd,de->mte", tokens.astype(jnp.float32), router.astype(jnp.float32))
    chosen = jnp.take_along_axis(logits, routes, axis=-1)
    logit_gap = chosen[..., 0] - chosen[..., 1]
    first_gate = jax.nn.sigmoid(logit_gap)
    second_gate = jax.nn.sigmoid(-logit_gap)
    hidden_blocks = tokens.reshape(blocks, TOK_DEV, D)
    route_blocks = routes.reshape(blocks, TOK_DEV, 2)
    target = jax.vmap(lambda one_block: route_targets(one_block, experts, capacity))(route_blocks)

    def place(block_rows, block_target):
        buffer_rows = jnp.zeros((experts * capacity, D), jnp.bfloat16)
        buffer_rows = buffer_rows.at[block_target[:, 0]].set(block_rows)
        return buffer_rows.at[block_target[:, 1]].set(block_rows)

    buffers = jax.vmap(place)(hidden_blocks, target)
    per_expert = buffers.reshape(blocks, experts, capacity, D).transpose(1, 0, 2, 3).reshape(experts, blocks * capacity, D)
    results = lax.map(expert_pass, (per_expert, gate_weight, up_weight, down_weight))
    back_rows = results.reshape(experts, blocks, capacity, D).transpose(1, 0, 2, 3).reshape(blocks, experts * capacity, D)
    first_rows = jax.vmap(lambda b_rows, b_target: jnp.take(b_rows, b_target[:, 0], axis=0))(back_rows, target)
    second_rows = jax.vmap(lambda b_rows, b_target: jnp.take(b_rows, b_target[:, 1], axis=0))(back_rows, target)
    first_rows = first_rows.reshape(MB, TOKENS, D).astype(jnp.float32)
    second_rows = second_rows.reshape(MB, TOKENS, D).astype(jnp.float32)
    layer_out = (tokens.astype(jnp.float32) + first_gate[..., None] * first_rows + second_gate[..., None] * second_rows).astype(jnp.bfloat16)

    gram_scale = experts / (2.0 * MB * TOKENS)
    replica_rows = per_expert.reshape(experts, MB, N_EXPERT, N_DP, capacity, D).transpose(0, 3, 1, 2, 4, 5)
    replica_rows = replica_rows.reshape(experts, N_DP, MB * N_EXPERT * capacity, D)

    def gram_pass(rows_of_expert):
        as_float = rows_of_expert.astype(jnp.float32)
        partial_value = (jnp.einsum("nrd,nrf->ndf", as_float, as_float) * gram_scale).astype(jnp.bfloat16)
        partial_value = lax.optimization_barrier(partial_value)
        return jnp.sum(partial_value.astype(jnp.float32), axis=0).astype(jnp.bfloat16)

    grams = lax.map(gram_pass, replica_rows)
    return layer_out, grams
```

```python
import jax
import jax.numpy as jnp
from jax import lax
from jax.sharding import PartitionSpec as P


def route_targets(route_ids, experts, capacity):
    onehot = (route_ids[:, :, None] == jnp.arange(experts, dtype=jnp.int32)[None, None, :]).astype(
        jnp.int32
    )
    flattened = onehot.reshape(-1, experts)
    pairs = jnp.arange(flattened.shape[0], dtype=jnp.int32)
    earlier = (pairs[None, :] < pairs[:, None]).astype(jnp.bfloat16)
    before = jnp.dot(
        earlier, flattened.astype(jnp.bfloat16), preferred_element_type=jnp.float32
    ).astype(jnp.int32)
    slot_rank = jnp.sum(before * flattened, axis=1).reshape(route_ids.shape)
    return route_ids * capacity + slot_rank


def on_device(tokens, routes, router, gate_weight, up_weight, down_weight):
    micro_count = tokens.shape[0]
    rows_dev = tokens.shape[1]
    model_width = tokens.shape[2]
    experts = router.shape[1]
    capacity = 9 * rows_dev // (4 * experts)
    section_count = lax.axis_size("section")
    replicas = lax.axis_size("dp")
    section_index = lax.axis_index("section")
    col_width = model_width // section_count
    gate_rows = gate_weight[0]
    up_rows = up_weight[0]
    down_rows = down_weight[0]
    logits = jnp.einsum("mtd,de->mte", tokens, router, preferred_element_type=jnp.float32)
    chosen = jnp.take_along_axis(logits, routes, axis=-1)
    logit_gap = chosen[..., 0] - chosen[..., 1]
    first_gate = jax.nn.sigmoid(logit_gap)
    second_gate = jax.nn.sigmoid(-logit_gap)
    target = jax.vmap(lambda one_block: route_targets(one_block, experts, capacity))(routes)
    slot_ids = jnp.arange(experts * capacity, dtype=jnp.int32)
    placing = jnp.sum(
        (slot_ids[None, :, None, None] == target[:, None, :, :]).astype(jnp.float32), axis=3
    ).astype(jnp.bfloat16)
    outgoing = jnp.einsum(
        "mst,mtd->msd", placing, tokens, preferred_element_type=jnp.float32
    ).astype(jnp.bfloat16)
    outgoing = outgoing.reshape(micro_count, experts, capacity, model_width)
    arrived = lax.all_to_all(outgoing, "expert", split_axis=1, concat_axis=1, tiled=True)
    rows_all = arrived.reshape(-1, model_width)
    rows_both = lax.all_gather(rows_all, "dp", axis=0, tiled=True)
    gate_part = lax.dot_general(
        rows_both, gate_rows, (((1,), (1,)), ((), ())), preferred_element_type=jnp.float32
    )
    up_part = lax.dot_general(
        rows_both, up_rows, (((1,), (1,)), ((), ())), preferred_element_type=jnp.float32
    )
    inner_units = (jax.nn.silu(gate_part) * up_part).astype(jnp.bfloat16)
    partial_out = jnp.dot(inner_units, down_rows, preferred_element_type=jnp.float32)
    summed_out = lax.psum_scatter(
        partial_out.astype(jnp.bfloat16), "section", scatter_dimension=1, tiled=True
    )
    summed_out = lax.psum_scatter(summed_out, "dp", scatter_dimension=0, tiled=True)
    expert_out = summed_out.reshape(micro_count, experts, capacity, col_width)
    returned = lax.all_to_all(expert_out, "expert", split_axis=1, concat_axis=1, tiled=True)
    flat_back = returned.reshape(micro_count, experts * capacity, col_width)
    first_rows = jnp.take_along_axis(flat_back, target[:, :, 0][:, :, None], axis=1).astype(
        jnp.float32
    )
    second_rows = jnp.take_along_axis(flat_back, target[:, :, 1][:, :, None], axis=1).astype(
        jnp.float32
    )
    own_cols = lax.dynamic_slice_in_dim(tokens, section_index * col_width, col_width, 2).astype(
        jnp.float32
    )
    layer_out = (
        own_cols + first_gate[..., None] * first_rows + second_gate[..., None] * second_rows
    ).astype(jnp.bfloat16)
    all_tokens = rows_dev * lax.axis_size("expert") * replicas
    gram_scale = experts / (2.0 * micro_count * all_tokens)
    block_rows = col_width // replicas
    per_replica = rows_both.reshape(replicas, -1, model_width)
    left_cols = lax.dynamic_slice_in_dim(
        per_replica, (section_index * replicas + lax.axis_index("dp")) * block_rows, block_rows, 2
    )
    product = (
        jnp.einsum("nrd,nrf->ndf", left_cols, per_replica, preferred_element_type=jnp.float32)
        * gram_scale
    )
    rounded = lax.optimization_barrier(product.astype(jnp.bfloat16))
    gram_block = jnp.sum(rounded.astype(jnp.float32), axis=0).astype(jnp.bfloat16)
    return (layer_out, gram_block[None])


def solution(mesh):
    return jax.shard_map(
        on_device,
        mesh=mesh,
        in_specs=(
            P(None, ("expert", "dp"), None),
            P(None, ("expert", "dp"), None),
            P(),
            P("expert", ("section", "dp"), None),
            P("expert", ("section", "dp"), None),
            P("expert", ("section", "dp"), None),
        ),
        out_specs=(P(None, ("expert", "dp"), "section"), P("expert", ("section", "dp"), None)),
        check_vma=False,
    )
```

```python
import functools
import jax
import jax.numpy as jnp
from jax import lax
from jax.experimental import pallas as pl
from jax.experimental.pallas import tpu as pltpu
from jax.sharding import PartitionSpec as P


def route_targets(route_ids, experts, capacity):
    onehot = (route_ids[:, :, None] == jnp.arange(experts, dtype=jnp.int32)[None, None, :]).astype(
        jnp.int32
    )
    flattened = onehot.reshape(-1, experts)
    pairs = jnp.arange(flattened.shape[0], dtype=jnp.int32)
    earlier = (pairs[None, :] < pairs[:, None]).astype(jnp.bfloat16)
    before = jnp.dot(
        earlier, flattened.astype(jnp.bfloat16), preferred_element_type=jnp.float32
    ).astype(jnp.int32)
    slot_rank = jnp.sum(before * flattened, axis=1).reshape(route_ids.shape)
    return route_ids * capacity + slot_rank


def on_device(tokens, routes, router, gate_weight, up_weight, down_weight):
    micro_count = tokens.shape[0]
    rows_dev = tokens.shape[1]
    model_width = tokens.shape[2]
    experts = router.shape[1]
    capacity = 9 * rows_dev // (4 * experts)
    section_count = lax.axis_size("section")
    replicas = lax.axis_size("dp")
    section_index = lax.axis_index("section")
    col_width = model_width // section_count
    gate_rows = gate_weight[0]
    up_rows = up_weight[0]
    down_rows = down_weight[0]
    logits = jnp.einsum("mtd,de->mte", tokens, router, preferred_element_type=jnp.float32)
    chosen = jnp.take_along_axis(logits, routes, axis=-1)
    logit_gap = chosen[..., 0] - chosen[..., 1]
    first_gate = jax.nn.sigmoid(logit_gap)
    second_gate = jax.nn.sigmoid(-logit_gap)
    target = jax.vmap(lambda one_block: route_targets(one_block, experts, capacity))(routes)
    slot_ids = jnp.arange(experts * capacity, dtype=jnp.int32)
    placing = jnp.sum(
        (slot_ids[None, :, None, None] == target[:, None, :, :]).astype(jnp.float32), axis=3
    ).astype(jnp.bfloat16)
    outgoing = jnp.einsum(
        "mst,mtd->msd", placing, tokens, preferred_element_type=jnp.float32
    ).astype(jnp.bfloat16)
    outgoing = outgoing.reshape(micro_count, experts, capacity, model_width)
    arrived = lax.all_to_all(outgoing, "expert", split_axis=1, concat_axis=1, tiled=True)
    rows_all = arrived.reshape(-1, model_width)
    rows_both = lax.all_gather(rows_all, "dp", axis=0, tiled=True)
    gate_part = lax.dot_general(
        rows_both, gate_rows, (((1,), (1,)), ((), ())), preferred_element_type=jnp.float32
    )
    up_part = lax.dot_general(
        rows_both, up_rows, (((1,), (1,)), ((), ())), preferred_element_type=jnp.float32
    )
    inner_units = (jax.nn.silu(gate_part) * up_part).astype(jnp.bfloat16)
    partial_out = jnp.dot(inner_units, down_rows, preferred_element_type=jnp.float32)
    summed_out = lax.psum_scatter(
        partial_out.astype(jnp.bfloat16), "section", scatter_dimension=1, tiled=True
    )
    summed_out = lax.psum_scatter(summed_out, "dp", scatter_dimension=0, tiled=True)
    expert_out = summed_out.reshape(micro_count, experts, capacity, col_width)
    returned = lax.all_to_all(expert_out, "expert", split_axis=1, concat_axis=1, tiled=True)
    flat_back = returned.reshape(micro_count, experts * capacity, col_width)
    first_rows = jnp.take_along_axis(flat_back, target[:, :, 0][:, :, None], axis=1).astype(
        jnp.float32
    )
    second_rows = jnp.take_along_axis(flat_back, target[:, :, 1][:, :, None], axis=1).astype(
        jnp.float32
    )
    own_cols = lax.dynamic_slice_in_dim(tokens, section_index * col_width, col_width, 2).astype(
        jnp.float32
    )
    layer_out = (
        own_cols + first_gate[..., None] * first_rows + second_gate[..., None] * second_rows
    ).astype(jnp.bfloat16)
    all_tokens = rows_dev * lax.axis_size("expert") * replicas
    gram_scale = experts / (2.0 * micro_count * all_tokens)
    block_rows = col_width // replicas
    per_replica = rows_both.reshape(replicas, -1, model_width)
    left_cols = lax.dynamic_slice_in_dim(
        per_replica, (section_index * replicas + lax.axis_index("dp")) * block_rows, block_rows, 2
    )
    product = (
        jnp.einsum("nrd,nrf->ndf", left_cols, per_replica, preferred_element_type=jnp.float32)
        * gram_scale
    )
    rounded = lax.optimization_barrier(product.astype(jnp.bfloat16))
    gram_block = jnp.sum(rounded.astype(jnp.float32), axis=0).astype(jnp.bfloat16)
    return (layer_out, gram_block[None])


BF16, F32 = jnp.bfloat16, jnp.float32


def expert_kernel(
    experts, rows, scale, ob, gate_hbm, up_hbm, down_hbm, ret, gram,
    xin, gate_v, up_v, down_v, inner, part, from_core, to_x, from_x, to_y, from_y, final, left_t,
    w_sem, l_sem, z_s, z_r, y_s, y_r, x_s, x_r, c_s, c_r, d_s, d_r, rc_s, rc_r, rx_s, rx_r, ry_s, ry_r, rz_s, rz_r,
):
    width = ob.shape[2]
    half, third = width // 2, width // 6
    part_cols = width // 4
    s, e, d = lax.axis_index("section"), lax.axis_index("expert"), lax.axis_index("dp")
    x, c = s // 2, s % 2
    core_nb = {"section": x * 2 + 1 - c}
    x_nb = {"section": (1 - x) * 2 + c}
    y_nb = {"dp": 1 - d}
    z_nb = [{"expert": (e + k) % experts} for k in range(experts)]
    sent = []

    def put(src, dst, send, recv, to):
        copy = pltpu.make_async_remote_copy(
            src_ref=src, dst_ref=dst, send_sem=send, recv_sem=recv,
            device_id=to, device_id_type=pl.DeviceIdType.MESH,
        )
        copy.start()
        sent.append(copy)

    def got(dst, send, recv, to):
        pltpu.make_async_remote_copy(
            src_ref=dst, dst_ref=dst, send_sem=send, recv_sem=recv,
            device_id=to, device_id_type=pl.DeviceIdType.MESH,
        ).wait_recv()

    weights = [
        pltpu.make_async_copy(gate_hbm, gate_v, w_sem.at[0]),
        pltpu.make_async_copy(up_hbm, up_v, w_sem.at[1]),
        pltpu.make_async_copy(down_hbm, down_v, w_sem.at[2]),
    ]
    for copy in weights:
        copy.start()
    row_of = lambda src: pl.ds(pl.multiple_of(src * rows, 16), rows)
    own_copy = pltpu.make_async_copy(ob.at[e], xin.at[d, row_of(e)], l_sem)
    own_copy.start()

    barrier = pltpu.get_barrier_semaphore()
    partners = [core_nb, x_nb, y_nb] + z_nb[1:]
    for to in partners:
        pl.semaphore_signal(barrier, inc=1, device_id=to, device_id_type=pl.DeviceIdType.MESH)
    pl.semaphore_wait(barrier, len(partners))

    fetched = pl.ds(pl.multiple_of(c * half + x * third, 128), 2 * third)
    mine_x = pl.ds(pl.multiple_of(c * half + x * 2 * third, 128), third)
    theirs_x = pl.ds(pl.multiple_of(c * half + (1 - x) * 2 * third, 128), third)
    core_fetched = pl.ds(pl.multiple_of((1 - c) * half + x * third, 128), 2 * third)
    core_x = pl.ds(pl.multiple_of((1 - c) * half + (1 - x) * 2 * third, 128), third)
    came = [(e + experts - k) % experts for k in range(experts)]

    def at(own, k, cols):
        return xin.at[d if own else 1 - d, row_of(came[k]), cols]

    for k in range(1, experts):
        put(
            ob.at[(e + k) % experts, :, fetched], xin.at[d, row_of(e), fetched],
            z_s.at[k], z_r.at[k], z_nb[k],
        )
    put(ob.at[e, :, fetched], xin.at[d, row_of(e), fetched], y_s.at[0], y_r.at[0], y_nb)
    for k in range(1, experts):
        got(at(True, k, fetched), z_s.at[k], z_r.at[k], z_nb[k])
        put(at(True, k, fetched), at(True, k, fetched), y_s.at[k], y_r.at[k], y_nb)
        put(at(True, k, mine_x), at(True, k, mine_x), x_s.at[0, k], x_r.at[0, k], x_nb)
        put(at(True, k, fetched), at(True, k, fetched), c_s.at[0, k], c_r.at[0, k], core_nb)
    for k in range(1, experts):
        got(at(True, k, theirs_x), x_s.at[0, k], x_r.at[0, k], x_nb)
        put(at(True, k, theirs_x), at(True, k, theirs_x), d_s.at[0, k], d_r.at[0, k], core_nb)

    def y_arrival(k):
        got(at(False, k, fetched), y_s.at[k], y_r.at[k], y_nb)
        put(at(False, k, mine_x), at(False, k, mine_x), x_s.at[1, k], x_r.at[1, k], x_nb)
        put(at(False, k, fetched), at(False, k, fetched), c_s.at[1, k], c_r.at[1, k], core_nb)

    def all_here(p):
        for k in range(1 - p, experts):
            own = p == 0
            got(at(own, k, core_fetched), c_s.at[p, k], c_r.at[p, k], core_nb)
            got(at(own, k, core_x), d_s.at[p, k], d_r.at[p, k], core_nb)

    tile = 256
    steps = gate_v.shape[0] // tile

    def hidden(which, h):
        place = pl.ds(pl.multiple_of(h * tile, tile), tile)
        nt = (((1,), (1,)), ((), ()))
        g = lax.dot_general(xin[which], gate_v[place, :], nt, preferred_element_type=F32)
        u = lax.dot_general(xin[which], up_v[place, :], nt, preferred_element_type=F32)
        inner[:, place] = (g / (1.0 + jnp.exp(-g)) * u).astype(BF16)

    def outputs(p, section):
        def step(j, carry):
            place = pl.ds(pl.multiple_of(j * tile, tile), tile)
            cols = pl.ds(pl.multiple_of(section * part_cols + j * tile, tile), tile)
            part[p, section, :, place] = jnp.dot(
                inner[...], down_v[:, cols], preferred_element_type=F32
            ).astype(BF16)
            return carry

        lax.fori_loop(0, part_cols // tile, step, 0)

    def project(p):
        for far in (0, 1):
            block = ((1 - x) if far == 0 else x)
            outputs(p, 2 * block + 1 - c)
            put(
                part.at[p, 2 * block + 1 - c], from_core.at[p, far],
                rc_s.at[p, far], rc_r.at[p, far], core_nb,
            )
        outputs(p, 2 * (1 - x) + c)
        outputs(p, 2 * x + c)

    chunks = list(range(1, experts)) + [0]

    def send_x(p):
        got(from_core.at[p, 0], rc_s.at[p, 0], rc_r.at[p, 0], core_nb)
        for k in chunks:
            r = row_of((e + k) % experts)
            to_x[p, r, :] = (
                part[p, 2 * (1 - x) + c, r, :].astype(F32) + from_core[p, 0, r, :].astype(F32)
            ).astype(BF16)
            put(to_x.at[p, r], from_x.at[p, r], rx_s.at[p, k], rx_r.at[p, k], x_nb)

    own_copy.wait()
    for copy in weights:
        copy.wait()
    all_here(0)
    for k in range(experts):
        if k < steps:
            hidden(d, k)
        y_arrival(k)
    for h in range(experts, steps):
        hidden(d, h)
    project(0)
    for k in range(experts):
        got(at(False, k, theirs_x), x_s.at[1, k], x_r.at[1, k], x_nb)
        put(at(False, k, theirs_x), at(False, k, theirs_x), d_s.at[1, k], d_r.at[1, k], core_nb)
    send_x(0)
    all_here(1)

    def hidden_step(h, carry):
        hidden(1 - d, h)
        return carry

    lax.fori_loop(0, steps, hidden_step, 0)
    project(1)
    send_x(1)

    block_rows = gram.shape[0]
    left = pl.ds(pl.multiple_of((s * 2 + d) * block_rows, 128), block_rows)
    for r in (0, 1):
        left_t[r] = xin[r, :, left].astype(F32).T.astype(BF16)

    def gram_step(j, carry):
        place = pl.ds(pl.multiple_of(j * tile, tile), tile)
        total = jnp.zeros((block_rows, tile), F32)
        for r in (0, 1):
            one = jnp.dot(left_t[r], xin[r, :, place], preferred_element_type=F32) * scale
            total = total + one.astype(BF16).astype(F32)
        gram[:, place] = total.astype(BF16)
        return carry

    lax.fori_loop(0, width // tile, gram_step, 0)

    got(from_core.at[1, 1], rc_s.at[1, 1], rc_r.at[1, 1], core_nb)
    for k in chunks:
        r = row_of((e + k) % experts)
        got(from_x.at[1, r], rx_s.at[1, k], rx_r.at[1, k], x_nb)
        to_y[r, :] = (
            part[1, 2 * x + c, r, :].astype(F32)
            + from_core[1, 1, r, :].astype(F32)
            + from_x[1, r, :].astype(F32)
        ).astype(BF16)
        put(to_y.at[r], from_y.at[r], ry_s.at[k], ry_r.at[k], y_nb)
    got(from_core.at[0, 1], rc_s.at[0, 1], rc_r.at[0, 1], core_nb)
    for k in chunks:
        r = row_of((e + k) % experts)
        got(from_x.at[0, r], rx_s.at[0, k], rx_r.at[0, k], x_nb)
        got(from_y.at[r], ry_s.at[k], ry_r.at[k], y_nb)
        value = (
            part[0, 2 * x + c, r, :].astype(F32)
            + from_core[0, 1, r, :].astype(F32)
            + from_x[0, r, :].astype(F32)
            + from_y[r, :].astype(F32)
        ).astype(BF16)
        if k == 0:
            ret[e] = value
        else:
            final[k] = value
            put(final.at[k], ret.at[e], rz_s.at[k], rz_r.at[k], z_nb[k])
    for k in range(1, experts):
        got(ret.at[came[k]], rz_s.at[k], rz_r.at[k], z_nb[k])
    for copy in sent:
        copy.wait_send()


def expert_call(ob, gate_rows, up_rows, down_rows, block_rows, scale):
    experts, rows, width = ob.shape
    hidden_rows = gate_rows.shape[0]
    every = experts * rows
    cols = width // 4
    dma = pltpu.SemaphoreType.DMA
    vmem = pl.BlockSpec(memory_space=pltpu.VMEM)
    hbm = pl.BlockSpec(memory_space=pl.ANY)
    return pl.pallas_call(
        functools.partial(expert_kernel, experts, rows, scale),
        out_shape=(
            jax.ShapeDtypeStruct((experts, rows, cols), BF16),
            jax.ShapeDtypeStruct((block_rows, width), BF16),
        ),
        in_specs=[vmem, hbm, hbm, hbm],
        out_specs=(vmem, vmem),
        scratch_shapes=[
            pltpu.VMEM((2, every, width), BF16),
            pltpu.VMEM((hidden_rows, width), BF16),
            pltpu.VMEM((hidden_rows, width), BF16),
            pltpu.VMEM((hidden_rows, width), BF16),
            pltpu.VMEM((every, hidden_rows), BF16),
            pltpu.VMEM((2, 4, every, cols), BF16),
            pltpu.VMEM((2, 2, every, cols), BF16),
            pltpu.VMEM((2, every, cols), BF16),
            pltpu.VMEM((2, every, cols), BF16),
            pltpu.VMEM((every, cols), BF16),
            pltpu.VMEM((every, cols), BF16),
            pltpu.VMEM((experts, rows, cols), BF16),
            pltpu.VMEM((2, block_rows, every), BF16),
            dma((3,)), dma,
            dma((experts,)), dma((experts,)), dma((experts,)), dma((experts,)),
            dma((2, experts)), dma((2, experts)), dma((2, experts)), dma((2, experts)),
            dma((2, experts)), dma((2, experts)),
            dma((2, 2)), dma((2, 2)), dma((2, experts)), dma((2, experts)),
            dma((experts,)), dma((experts,)), dma((experts,)), dma((experts,)),
        ],
        compiler_params=pltpu.CompilerParams(
            collective_id=0, has_side_effects=True, vmem_limit_bytes=56 * 1024 * 1024
        ),
    )(ob, gate_rows, up_rows, down_rows)


def on_device_fused(tokens, routes, router, gate_weight, up_weight, down_weight):
    micro_count, rows_dev, model_width = tokens.shape
    experts = router.shape[1]
    capacity = 9 * rows_dev // (4 * experts)
    padded = -(-capacity // 8) * 8
    section_count = lax.axis_size("section")
    replicas = lax.axis_size("dp")
    col_width = model_width // section_count
    logits = jnp.einsum("mtd,de->mte", tokens, router, preferred_element_type=F32)
    named = routes[..., None] == jnp.arange(experts, dtype=jnp.int32)
    chosen = jnp.sum(jnp.where(named, logits[:, :, None, :], 0.0), axis=-1)
    logit_gap = chosen[..., 0] - chosen[..., 1]
    first_gate = jax.nn.sigmoid(logit_gap)
    second_gate = jax.nn.sigmoid(-logit_gap)
    target = jax.vmap(lambda one_block: route_targets(one_block, experts, padded))(routes)
    hot = (
        jnp.arange(experts * padded, dtype=jnp.int32).reshape(experts, 1, 1, padded, 1)
        == target.transpose(2, 0, 1)[None, :, :, None, :]
    )
    placing = (hot[:, 0] | hot[:, 1]).astype(BF16)
    outgoing = jnp.einsum("emst,mtd->emsd", placing, tokens, preferred_element_type=F32)
    outgoing = outgoing.astype(BF16).reshape(experts, micro_count * padded, model_width)
    all_tokens = rows_dev * lax.axis_size("expert") * replicas
    gram_scale = experts / (2.0 * micro_count * all_tokens)
    returned, gram_block = expert_call(
        outgoing, gate_weight[0], up_weight[0], down_weight[0], col_width // replicas, gram_scale
    )
    back = returned.reshape(experts, micro_count, padded, col_width)
    picked = jnp.einsum(
        "ekmst,emsd->kmtd", hot.astype(BF16), back, preferred_element_type=F32
    )
    own_cols = lax.dynamic_slice_in_dim(
        tokens, lax.axis_index("section") * col_width, col_width, 2
    ).astype(F32)
    layer_out = (
        own_cols + first_gate[..., None] * picked[0] + second_gate[..., None] * picked[1]
    ).astype(BF16)
    return (layer_out, gram_block[None])


def solution(mesh):
    sizes = dict(mesh.shape)
    fused = sizes["section"] == 4 and sizes["dp"] == 2
    return jax.shard_map(
        on_device_fused if fused else on_device,
        mesh=mesh,
        in_specs=(
            P(None, ("expert", "dp"), None),
            P(None, ("expert", "dp"), None),
            P(),
            P("expert", ("section", "dp"), None),
            P("expert", ("section", "dp"), None),
            P("expert", ("section", "dp"), None),
        ),
        out_specs=(P(None, ("expert", "dp"), "section"), P("expert", ("section", "dp"), None)),
        check_vma=False,
    )
```

```python
import functools
import jax
import jax.numpy as jnp
from jax import lax
from jax.experimental import pallas as pl
from jax.experimental.pallas import tpu as pltpu
from jax.sharding import PartitionSpec as P


def route_targets(route_ids, experts, capacity):
    onehot = (route_ids[:, :, None] == jnp.arange(experts, dtype=jnp.int32)[None, None, :]).astype(
        jnp.int32
    )
    flattened = onehot.reshape(-1, experts)
    pairs = jnp.arange(flattened.shape[0], dtype=jnp.int32)
    earlier = (pairs[None, :] < pairs[:, None]).astype(jnp.bfloat16)
    before = jnp.dot(
        earlier, flattened.astype(jnp.bfloat16), preferred_element_type=jnp.float32
    ).astype(jnp.int32)
    slot_rank = jnp.sum(before * flattened, axis=1).reshape(route_ids.shape)
    return route_ids * capacity + slot_rank


def on_device(tokens, routes, router, gate_weight, up_weight, down_weight):
    micro_count = tokens.shape[0]
    rows_dev = tokens.shape[1]
    model_width = tokens.shape[2]
    experts = router.shape[1]
    capacity = 9 * rows_dev // (4 * experts)
    section_count = lax.axis_size("section")
    replicas = lax.axis_size("dp")
    section_index = lax.axis_index("section")
    col_width = model_width // section_count
    gate_rows = gate_weight[0]
    up_rows = up_weight[0]
    down_rows = down_weight[0]
    logits = jnp.einsum("mtd,de->mte", tokens, router, preferred_element_type=jnp.float32)
    chosen = jnp.take_along_axis(logits, routes, axis=-1)
    logit_gap = chosen[..., 0] - chosen[..., 1]
    first_gate = jax.nn.sigmoid(logit_gap)
    second_gate = jax.nn.sigmoid(-logit_gap)
    target = jax.vmap(lambda one_block: route_targets(one_block, experts, capacity))(routes)
    slot_ids = jnp.arange(experts * capacity, dtype=jnp.int32)
    placing = jnp.sum(
        (slot_ids[None, :, None, None] == target[:, None, :, :]).astype(jnp.float32), axis=3
    ).astype(jnp.bfloat16)
    outgoing = jnp.einsum(
        "mst,mtd->msd", placing, tokens, preferred_element_type=jnp.float32
    ).astype(jnp.bfloat16)
    outgoing = outgoing.reshape(micro_count, experts, capacity, model_width)
    arrived = lax.all_to_all(outgoing, "expert", split_axis=1, concat_axis=1, tiled=True)
    rows_all = arrived.reshape(-1, model_width)
    rows_both = lax.all_gather(rows_all, "dp", axis=0, tiled=True)
    gate_part = lax.dot_general(
        rows_both, gate_rows, (((1,), (1,)), ((), ())), preferred_element_type=jnp.float32
    )
    up_part = lax.dot_general(
        rows_both, up_rows, (((1,), (1,)), ((), ())), preferred_element_type=jnp.float32
    )
    inner_units = (jax.nn.silu(gate_part) * up_part).astype(jnp.bfloat16)
    partial_out = jnp.dot(inner_units, down_rows, preferred_element_type=jnp.float32)
    summed_out = lax.psum_scatter(
        partial_out.astype(jnp.bfloat16), "section", scatter_dimension=1, tiled=True
    )
    summed_out = lax.psum_scatter(summed_out, "dp", scatter_dimension=0, tiled=True)
    expert_out = summed_out.reshape(micro_count, experts, capacity, col_width)
    returned = lax.all_to_all(expert_out, "expert", split_axis=1, concat_axis=1, tiled=True)
    flat_back = returned.reshape(micro_count, experts * capacity, col_width)
    first_rows = jnp.take_along_axis(flat_back, target[:, :, 0][:, :, None], axis=1).astype(
        jnp.float32
    )
    second_rows = jnp.take_along_axis(flat_back, target[:, :, 1][:, :, None], axis=1).astype(
        jnp.float32
    )
    own_cols = lax.dynamic_slice_in_dim(tokens, section_index * col_width, col_width, 2).astype(
        jnp.float32
    )
    layer_out = (
        own_cols + first_gate[..., None] * first_rows + second_gate[..., None] * second_rows
    ).astype(jnp.bfloat16)
    all_tokens = rows_dev * lax.axis_size("expert") * replicas
    gram_scale = experts / (2.0 * micro_count * all_tokens)
    block_rows = col_width // replicas
    per_replica = rows_both.reshape(replicas, -1, model_width)
    left_cols = lax.dynamic_slice_in_dim(
        per_replica, (section_index * replicas + lax.axis_index("dp")) * block_rows, block_rows, 2
    )
    product = (
        jnp.einsum("nrd,nrf->ndf", left_cols, per_replica, preferred_element_type=jnp.float32)
        * gram_scale
    )
    rounded = lax.optimization_barrier(product.astype(jnp.bfloat16))
    gram_block = jnp.sum(rounded.astype(jnp.float32), axis=0).astype(jnp.bfloat16)
    return (layer_out, gram_block[None])


BF16, F32 = jnp.bfloat16, jnp.float32


def expert_kernel(
    experts, rows, scale, ob, gate_hbm, up_hbm, down_hbm, ret, gram_hbm,
    xin, gate_v, up_v, down_v, inner, part, from_core, to_x, from_x, to_y, from_y, final, left_t, gram,
    w_sem, l_sem, g_sem, z_s, z_r, y_s, y_r, x_s, x_r, c_s, c_r, d_s, d_r, rc_s, rc_r, rx_s, rx_r, ry_s, ry_r, rz_s, rz_r,
):
    width = ob.shape[2]
    half, third = width // 2, width // 6
    part_cols = width // 4
    s, e, d = lax.axis_index("section"), lax.axis_index("expert"), lax.axis_index("dp")
    x, c = s // 2, s % 2
    core_nb = {"section": x * 2 + 1 - c}
    x_nb = {"section": (1 - x) * 2 + c}
    y_nb = {"dp": 1 - d}
    z_nb = [{"expert": (e + k) % experts} for k in range(experts)]
    sent = []

    def put(src, dst, send, recv, to):
        copy = pltpu.make_async_remote_copy(
            src_ref=src, dst_ref=dst, send_sem=send, recv_sem=recv,
            device_id=to, device_id_type=pl.DeviceIdType.MESH,
        )
        copy.start()
        sent.append(copy)

    def got(dst, send, recv, to):
        pltpu.make_async_remote_copy(
            src_ref=dst, dst_ref=dst, send_sem=send, recv_sem=recv,
            device_id=to, device_id_type=pl.DeviceIdType.MESH,
        ).wait_recv()

    weights = [
        pltpu.make_async_copy(gate_hbm, gate_v, w_sem.at[0]),
        pltpu.make_async_copy(up_hbm, up_v, w_sem.at[1]),
        pltpu.make_async_copy(down_hbm, down_v, w_sem.at[2]),
    ]
    for copy in weights:
        copy.start()
    row_of = lambda src: pl.ds(pl.multiple_of(src * rows, 16), rows)
    own_copy = pltpu.make_async_copy(ob.at[e], xin.at[d, row_of(e)], l_sem)
    own_copy.start()

    barrier = pltpu.get_barrier_semaphore()
    partners = [core_nb, x_nb, y_nb] + z_nb[1:]
    for to in partners:
        pl.semaphore_signal(barrier, inc=1, device_id=to, device_id_type=pl.DeviceIdType.MESH)
    pl.semaphore_wait(barrier, len(partners))

    fetched = pl.ds(pl.multiple_of(c * half + x * third, 128), 2 * third)
    mine_x = pl.ds(pl.multiple_of(c * half + x * 2 * third, 128), third)
    theirs_x = pl.ds(pl.multiple_of(c * half + (1 - x) * 2 * third, 128), third)
    core_fetched = pl.ds(pl.multiple_of((1 - c) * half + x * third, 128), 2 * third)
    core_x = pl.ds(pl.multiple_of((1 - c) * half + (1 - x) * 2 * third, 128), third)
    came = [(e + experts - k) % experts for k in range(experts)]

    def at(own, k, cols):
        return xin.at[d if own else 1 - d, row_of(came[k]), cols]

    for k in range(1, experts):
        put(
            ob.at[(e + k) % experts, :, fetched], xin.at[d, row_of(e), fetched],
            z_s.at[k], z_r.at[k], z_nb[k],
        )
    put(ob.at[e, :, fetched], xin.at[d, row_of(e), fetched], y_s.at[0], y_r.at[0], y_nb)
    for k in range(1, experts):
        got(at(True, k, fetched), z_s.at[k], z_r.at[k], z_nb[k])
        put(at(True, k, fetched), at(True, k, fetched), y_s.at[k], y_r.at[k], y_nb)
        put(at(True, k, mine_x), at(True, k, mine_x), x_s.at[0, k], x_r.at[0, k], x_nb)
        put(at(True, k, fetched), at(True, k, fetched), c_s.at[0, k], c_r.at[0, k], core_nb)
    for k in range(1, experts):
        got(at(True, k, theirs_x), x_s.at[0, k], x_r.at[0, k], x_nb)
        put(at(True, k, theirs_x), at(True, k, theirs_x), d_s.at[0, k], d_r.at[0, k], core_nb)

    def y_arrival(k):
        got(at(False, k, fetched), y_s.at[k], y_r.at[k], y_nb)
        put(at(False, k, mine_x), at(False, k, mine_x), x_s.at[1, k], x_r.at[1, k], x_nb)
        put(at(False, k, fetched), at(False, k, fetched), c_s.at[1, k], c_r.at[1, k], core_nb)

    def all_here(p):
        for k in range(1 - p, experts):
            own = p == 0
            got(at(own, k, core_fetched), c_s.at[p, k], c_r.at[p, k], core_nb)
            got(at(own, k, core_x), d_s.at[p, k], d_r.at[p, k], core_nb)

    tile = 256
    steps = gate_v.shape[0] // tile

    def hidden(which, h):
        place = pl.ds(pl.multiple_of(h * tile, tile), tile)
        nt = (((1,), (1,)), ((), ()))
        g = lax.dot_general(xin[which], gate_v[place, :], nt, preferred_element_type=F32)
        u = lax.dot_general(xin[which], up_v[place, :], nt, preferred_element_type=F32)
        inner[:, place] = (g / (1.0 + jnp.exp(-g)) * u).astype(BF16)

    def outputs(p, section):
        def step(j, carry):
            place = pl.ds(pl.multiple_of(j * tile, tile), tile)
            cols = pl.ds(pl.multiple_of(section * part_cols + j * tile, tile), tile)
            part[p, section, :, place] = jnp.dot(
                inner[...], down_v[:, cols], preferred_element_type=F32
            ).astype(BF16)
            return carry

        lax.fori_loop(0, part_cols // tile, step, 0)

    def project(p):
        for far in (0, 1):
            block = ((1 - x) if far == 0 else x)
            outputs(p, 2 * block + 1 - c)
            put(
                part.at[p, 2 * block + 1 - c], from_core.at[p, far],
                rc_s.at[p, far], rc_r.at[p, far], core_nb,
            )
        outputs(p, 2 * (1 - x) + c)
        outputs(p, 2 * x + c)

    chunks = list(range(1, experts)) + [0]

    def send_x(p):
        got(from_core.at[p, 0], rc_s.at[p, 0], rc_r.at[p, 0], core_nb)
        for k in chunks:
            r = row_of((e + k) % experts)
            to_x[p, r, :] = (
                part[p, 2 * (1 - x) + c, r, :].astype(F32) + from_core[p, 0, r, :].astype(F32)
            ).astype(BF16)
            put(to_x.at[p, r], from_x.at[p, r], rx_s.at[p, k], rx_r.at[p, k], x_nb)

    own_copy.wait()
    for copy in weights:
        copy.wait()
    all_here(0)
    for k in range(experts):
        if k < steps:
            hidden(d, k)
        y_arrival(k)
    for h in range(experts, steps):
        hidden(d, h)
    project(0)
    for k in range(experts):
        got(at(False, k, theirs_x), x_s.at[1, k], x_r.at[1, k], x_nb)
        put(at(False, k, theirs_x), at(False, k, theirs_x), d_s.at[1, k], d_r.at[1, k], core_nb)
    send_x(0)
    all_here(1)

    def hidden_step(h, carry):
        hidden(1 - d, h)
        return carry

    lax.fori_loop(0, steps, hidden_step, 0)
    project(1)
    send_x(1)

    block_rows = gram.shape[0]
    left = pl.ds(pl.multiple_of((s * 2 + d) * block_rows, 128), block_rows)
    for r in (0, 1):
        left_t[r] = xin[r, :, left].astype(F32).T.astype(BF16)

    def gram_step(j, carry):
        place = pl.ds(pl.multiple_of(j * tile, tile), tile)
        total = jnp.zeros((block_rows, tile), F32)
        for r in (0, 1):
            one = jnp.dot(left_t[r], xin[r, :, place], preferred_element_type=F32) * scale
            total = total + one.astype(BF16).astype(F32)
        gram[:, place] = total.astype(BF16)
        return carry

    lax.fori_loop(0, width // tile, gram_step, 0)
    gram_copy = pltpu.make_async_copy(gram, gram_hbm, g_sem)
    gram_copy.start()

    got(from_core.at[1, 1], rc_s.at[1, 1], rc_r.at[1, 1], core_nb)
    for k in chunks:
        r = row_of((e + k) % experts)
        got(from_x.at[1, r], rx_s.at[1, k], rx_r.at[1, k], x_nb)
        to_y[r, :] = (
            part[1, 2 * x + c, r, :].astype(F32)
            + from_core[1, 1, r, :].astype(F32)
            + from_x[1, r, :].astype(F32)
        ).astype(BF16)
        put(to_y.at[r], from_y.at[r], ry_s.at[k], ry_r.at[k], y_nb)
    got(from_core.at[0, 1], rc_s.at[0, 1], rc_r.at[0, 1], core_nb)
    for k in chunks:
        r = row_of((e + k) % experts)
        got(from_x.at[0, r], rx_s.at[0, k], rx_r.at[0, k], x_nb)
        got(from_y.at[r], ry_s.at[k], ry_r.at[k], y_nb)
        value = (
            part[0, 2 * x + c, r, :].astype(F32)
            + from_core[0, 1, r, :].astype(F32)
            + from_x[0, r, :].astype(F32)
            + from_y[r, :].astype(F32)
        ).astype(BF16)
        if k == 0:
            ret[e] = value
        else:
            final[k] = value
            put(final.at[k], ret.at[e], rz_s.at[k], rz_r.at[k], z_nb[k])
    for k in range(1, experts):
        got(ret.at[came[k]], rz_s.at[k], rz_r.at[k], z_nb[k])
    for copy in sent:
        copy.wait_send()
    gram_copy.wait()


def expert_call(ob, gate_rows, up_rows, down_rows, block_rows, scale):
    experts, rows, width = ob.shape
    hidden_rows = gate_rows.shape[0]
    every = experts * rows
    cols = width // 4
    dma = pltpu.SemaphoreType.DMA
    vmem = pl.BlockSpec(memory_space=pltpu.VMEM)
    hbm = pl.BlockSpec(memory_space=pl.ANY)
    return pl.pallas_call(
        functools.partial(expert_kernel, experts, rows, scale),
        out_shape=(
            jax.ShapeDtypeStruct((experts, rows, cols), BF16),
            jax.ShapeDtypeStruct((block_rows, width), BF16),
        ),
        in_specs=[vmem, hbm, hbm, hbm],
        out_specs=(vmem, hbm),
        scratch_shapes=[
            pltpu.VMEM((2, every, width), BF16),
            pltpu.VMEM((hidden_rows, width), BF16),
            pltpu.VMEM((hidden_rows, width), BF16),
            pltpu.VMEM((hidden_rows, width), BF16),
            pltpu.VMEM((every, hidden_rows), BF16),
            pltpu.VMEM((2, 4, every, cols), BF16),
            pltpu.VMEM((2, 2, every, cols), BF16),
            pltpu.VMEM((2, every, cols), BF16),
            pltpu.VMEM((2, every, cols), BF16),
            pltpu.VMEM((every, cols), BF16),
            pltpu.VMEM((every, cols), BF16),
            pltpu.VMEM((experts, rows, cols), BF16),
            pltpu.VMEM((2, block_rows, every), BF16),
            pltpu.VMEM((block_rows, width), BF16),
            dma((3,)), dma, dma,
            dma((experts,)), dma((experts,)), dma((experts,)), dma((experts,)),
            dma((2, experts)), dma((2, experts)), dma((2, experts)), dma((2, experts)),
            dma((2, experts)), dma((2, experts)),
            dma((2, 2)), dma((2, 2)), dma((2, experts)), dma((2, experts)),
            dma((experts,)), dma((experts,)), dma((experts,)), dma((experts,)),
        ],
        compiler_params=pltpu.CompilerParams(
            collective_id=0, has_side_effects=True, vmem_limit_bytes=56 * 1024 * 1024
        ),
    )(ob, gate_rows, up_rows, down_rows)


def on_device_fused(tokens, routes, router, gate_weight, up_weight, down_weight):
    micro_count, rows_dev, model_width = tokens.shape
    experts = router.shape[1]
    capacity = 9 * rows_dev // (4 * experts)
    padded = -(-capacity // 8) * 8
    section_count = lax.axis_size("section")
    replicas = lax.axis_size("dp")
    col_width = model_width // section_count
    logits = jnp.einsum("mtd,de->mte", tokens, router, preferred_element_type=F32)
    named = routes[..., None] == jnp.arange(experts, dtype=jnp.int32)
    chosen = jnp.sum(jnp.where(named, logits[:, :, None, :], 0.0), axis=-1)
    logit_gap = chosen[..., 0] - chosen[..., 1]
    first_gate = jax.nn.sigmoid(logit_gap)
    second_gate = jax.nn.sigmoid(-logit_gap)
    target = jax.vmap(lambda one_block: route_targets(one_block, experts, padded))(routes)
    micro = jnp.arange(micro_count, dtype=jnp.int32)[:, None, None]
    chosen_slot = target % padded
    wanted = ((routes * micro_count + micro) * padded + chosen_slot).reshape(-1, 2)
    places = jnp.arange(experts * micro_count * padded, dtype=jnp.int32)
    placing = (
        (places[:, None] == wanted[None, :, 0]) | (places[:, None] == wanted[None, :, 1])
    ).astype(BF16)
    outgoing = jnp.dot(
        placing, tokens.reshape(-1, model_width), preferred_element_type=F32
    ).astype(BF16).reshape(experts, micro_count * padded, model_width)
    all_tokens = rows_dev * lax.axis_size("expert") * replicas
    gram_scale = experts / (2.0 * micro_count * all_tokens)
    returned, gram_block = expert_call(
        outgoing, gate_weight[0], up_weight[0], down_weight[0], col_width // replicas, gram_scale
    )
    back = returned.reshape(-1, col_width)
    taking = (wanted.T[:, :, None] == places).astype(BF16).reshape(-1, places.shape[0])
    picked = jnp.dot(taking, back, preferred_element_type=F32)
    picked = picked.reshape(2, micro_count, rows_dev, col_width)
    own_cols = lax.dynamic_slice_in_dim(
        tokens, lax.axis_index("section") * col_width, col_width, 2
    ).astype(F32)
    layer_out = (
        own_cols + first_gate[..., None] * picked[0] + second_gate[..., None] * picked[1]
    ).astype(BF16)
    return (layer_out, gram_block[None])


def solution(mesh):
    sizes = dict(mesh.shape)
    fused = sizes["section"] == 4 and sizes["dp"] == 2
    return jax.shard_map(
        on_device_fused if fused else on_device,
        mesh=mesh,
        in_specs=(
            P(None, ("expert", "dp"), None),
            P(None, ("expert", "dp"), None),
            P(),
            P("expert", ("section", "dp"), None),
            P("expert", ("section", "dp"), None),
            P("expert", ("section", "dp"), None),
        ),
        out_specs=(P(None, ("expert", "dp"), "section"), P("expert", ("section", "dp"), None)),
        check_vma=False,
    )
```
